256 devices in a mesh: dp: 32 (over x_lo, z, core), slab: 8 (over y, x_hi).
Axes of the slice: x: 4 (x_hi: 2, x_lo: 2; x = x_hi * 2 + x_lo), y: 4, z: 8, core: 2. Of those that a mesh axis runs over, the one named last changes fastest.
Arguments:
- inputs: bfloat16 [32, 48, 36, 2048], P('dp', 'slab'), may hold values from -6 to 6
- weight: bfloat16 [3, 3, 2048, 256], replicated, may hold values from -0.046875 to 0.046875
- pre_norm: bfloat16 [32, 48, 36, 256], P('dp', 'slab'), may hold values from -50 to 50
- grad_norm: bfloat16 [32, 48, 36, 256], P('dp', 'slab'), may hold values from -6 to 6
- norm_gain: float32 [256], replicated, may hold values from 0.5 to 1.5
Outputs:
- input_grad: bfloat16 [32, 48, 36, 2048], P('dp', 'slab')
- weight_grad: float32 [3, 3, 2048, 256], P(None, None, ('dp', 'slab'))
- gain_grad: float32 [256], replicated
- bias_grad: float32 [256], replicated
The draws below stay inside these ranges and needn't reach their ends.
All inputs are finite; a program needn't handle non-finite values.
Results may differ from the reference program's by a relative error of at most 0.0049.
Values may be sent and summed in bfloat16 or wider, within the bound.
A program may use at most 128 MiB of HBM per device.

```python
import math
import jax
import jax.numpy as jnp
from jax import lax

CIN = 2048
OUTPUT_CHANNELS = 256
DILATION_STEP = 24
COLS = 36
IMAGES = 32
HEIGHT = 48


def draw_pre_norm(key, part):
    key = jax.random.fold_in(key, 7)
    key_base, key_chan, key_shift = jax.random.split(key, 3)
    array_shape = (IMAGES, HEIGHT, COLS, OUTPUT_CHANNELS)
    heights = jnp.arange(HEIGHT, dtype=jnp.float32)
    rising = jnp.exp(math.log(3.0) * heights / max(HEIGHT - 1, 1))
    base = jnp.clip(jax.random.normal(key_base, array_shape, jnp.float32), -4.0, 4.0)
    channel = jnp.exp(jax.random.uniform(key_chan, (OUTPUT_CHANNELS,), jnp.float32, math.log(0.5), math.log(4.0)))
    tap_displacement = jax.random.uniform(key_shift, (IMAGES, 1, 1, OUTPUT_CHANNELS), jnp.float32, -1.0, 1.0)
    tensor_values = tap_displacement + base * rising[None, :, None, None] * channel
    return tensor_values.astype(jnp.bfloat16)


def with_spikes(drawn, stream_key, source, target, shards_of, factor):
    def block_of(position):
        return (jnp.arange(drawn.shape[position]) // (drawn.shape[position] // shards_of)).reshape((-1,) + (1,) * (drawn.ndim - 1 - position))

    near = jax.random.permutation(stream_key, shards_of)[block_of(target)]
    far = (block_of(target) + shards_of // 2) % shards_of
    return jnp.where((block_of(source) == near) | (block_of(source) == far), factor * drawn, drawn)


def steps_of(own_key, shape, cuts, low, largest):
    level = 1.0
    for dim, blocks in cuts:
        draws = jax.random.uniform(jax.random.fold_in(jax.random.fold_in(own_key, 6), dim), (blocks,), jnp.float32, low / len(cuts), largest / len(cuts))
        level = level * jnp.repeat(jnp.exp(draws), shape[dim] // blocks).reshape((-1,) + (1,) * (len(shape) - 1 - dim))
    return level


def gaussian(key, shape, spread, bound, pieces=(), held_as=jnp.bfloat16):
    factor_of = steps_of(key, shape, pieces, -0.22, 0.18) if pieces else 1.0
    drawn = jax.random.normal(key, shape, jnp.float32) * spread * factor_of
    return jnp.minimum(jnp.maximum(drawn, -bound), bound).astype(held_as)


def gaussian_with(rng, dims, deviation, bound, cuts, heavy, kind=jnp.bfloat16):
    drawn = deviation * jax.random.normal(rng, dims, jnp.float32)
    if cuts:
        drawn = drawn * steps_of(rng, dims, cuts, -0.22, 0.18)
    return jnp.clip(with_spikes(drawn, jax.random.fold_in(rng, 3), *heavy), -bound, bound).astype(kind)


def setup_inputs(seed: int = 0) -> dict:
    key_list = jax.random.split(jax.random.key(seed), 6)
    inputs = gaussian_with(key_list[0], (IMAGES, HEIGHT, COLS, CIN), 1.0, 6.0, ((0, 32), (1, 8)), (0, 3, 32, 2.75))
    weight = gaussian(key_list[1], (3, 3, CIN, OUTPUT_CHANNELS), (9 * CIN) ** -0.5, 0.046875)
    pre_norm = draw_pre_norm(jax.random.fold_in(key_list[5], 71), 0)
    grad_norm = gaussian(key_list[3], (IMAGES, HEIGHT, COLS, OUTPUT_CHANNELS), 1.0, 6.0, ((0, 32), (1, 8)))
    norm_gain = jnp.clip(1.0 + 0.1 * jax.random.normal(key_list[4], (OUTPUT_CHANNELS,), jnp.float32), 0.5, 1.5)
    return {"inputs": inputs, "weight": weight, "pre_norm": pre_norm, "grad_norm": grad_norm, "norm_gain": norm_gain}


EPSILON = 1e-05

def displace_rows(tensor_values, tap_displacement):
    padded_input = jnp.pad(tensor_values, ((DILATION_STEP, DILATION_STEP), (0, 0), (0, 0)))
    return padded_input[DILATION_STEP + tap_displacement:DILATION_STEP + tap_displacement + tensor_values.shape[0]]

def displace_columns(tensor_values, tap_displacement):
    padded_input = jnp.pad(tensor_values, ((0, 0), (DILATION_STEP, DILATION_STEP), (0, 0)))
    return padded_input[:, DILATION_STEP + tap_displacement:DILATION_STEP + tap_displacement + tensor_values.shape[1]]

def reference(inputs, weight, pre_norm, grad_norm, norm_gain):
    cell_count = HEIGHT * COLS

    def per_image(running, items):
        image, saved, upstream = items
        saved_f = saved.astype(jnp.float32)
        mean_val = lax.optimization_barrier(jnp.sum(saved_f, axis=(0, 1))) / cell_count
        centred = saved_f - mean_val
        variance = lax.optimization_barrier(jnp.sum(centred * centred, axis=(0, 1))) / cell_count
        inv_std = lax.rsqrt(variance + EPSILON)
        zhat = centred * inv_std
        upstream_f = upstream.astype(jnp.float32)
        sum_g = lax.optimization_barrier(jnp.sum(upstream_f, axis=(0, 1)))
        sum_gz = lax.optimization_barrier(jnp.sum(upstream_f * zhat, axis=(0, 1)))
        gradient_before_norm = (norm_gain * inv_std * (upstream_f - sum_g / cell_count - zhat * (sum_gz / cell_count))).astype(jnp.bfloat16)
        flat_in = image.reshape(-1, CIN)
        grad_in = jnp.zeros((HEIGHT * COLS, CIN), jnp.float32)
        grads = []
        for row_kernel_tap in range(3):
            for column_kernel_tap in range(3):
                transferred_rows = displace_columns(displace_rows(gradient_before_norm, -(row_kernel_tap - 1) * DILATION_STEP), -(column_kernel_tap - 1) * DILATION_STEP).reshape(-1, OUTPUT_CHANNELS)
                grad_in = grad_in + jnp.dot(transferred_rows, weight[row_kernel_tap, column_kernel_tap].T, preferred_element_type=jnp.float32)
                grads.append(jnp.dot(flat_in.T, transferred_rows, preferred_element_type=jnp.float32))
        running = running + jnp.stack(grads).reshape(3, 3, CIN, OUTPUT_CHANNELS)
        return (running, (grad_in.astype(jnp.bfloat16).reshape(HEIGHT, COLS, CIN), sum_g, sum_gz))
    start = jnp.zeros((3, 3, CIN, OUTPUT_CHANNELS), jnp.float32)
    weight_grad, (input_grad, sum_g, sum_gz) = lax.scan(per_image, start, (inputs, pre_norm, grad_norm))
    return (input_grad, weight_grad, lax.optimization_barrier(jnp.sum(sum_gz, axis=0)), lax.optimization_barrier(jnp.sum(sum_g, axis=0)))
```

```python
import functools

import jax
import jax.numpy as jnp
from jax import lax
from jax.experimental import pallas as pl
from jax.experimental.pallas import tpu as pltpu
from jax.sharding import PartitionSpec as P

MESH = pl.DeviceIdType.MESH
F32 = jnp.float32
BF16 = jnp.bfloat16
EPSILON = 1e-05
TAPS = ((1, 1), (0, 1), (2, 1), (1, 0), (1, 2), (0, 0), (0, 2), (2, 0), (2, 2))


def kernel(
    sizes,
    x_hbm, w_hbm, pre_hbm, gn_hbm, gain_ref,
    gin_ref, wg_ref, gg_ref, bg_ref,
    pre_v, gn_v, st, xr, gr, xf, xc, gf, gc, wv, gin_v,
    dw, crecv, keep, xsend, xrecv, fsend, frecv,
    gb, gbc, gbk, gbx, gbs, gbf,
    load_sem, w_sem, x_loc, gin_sem, f_loc, gb_loc,
    st_s, st_r, x_s, x_r, g_s, g_r, c_s, c_r, l_s, l_r, f_s, f_r,
    gc_s, gc_r, gl_s, gl_r, gf_s, gf_r,
):
    ns, nz, rows, cols, cin, cout = sizes
    gran = cin // (2 * ns)
    pad = xf.shape[1]
    side = xc.shape[1]
    third = cols // 3
    cells = rows * cols * ns
    slab = lax.axis_index("slab")
    dp = lax.axis_index("dp")
    core = lax.rem(dp, 2)
    z = lax.rem(lax.div(dp, 2), nz)
    xlo = lax.div(dp, 2 * nz)
    other_core = {"dp": dp + 1 - 2 * core, "slab": slab}
    other_x = {"dp": dp + (1 - 2 * xlo) * (2 * nz), "slab": slab}
    own_final = z == slab

    def peer(q):
        return lax.rem(slab + q, ns)

    def source(q):
        return lax.rem(slab + ns - q, ns)

    def image_device(s):
        return {"dp": dp, "slab": s}

    def owner(q):
        return {"dp": (xlo * nz + slab) * 2 + core, "slab": lax.rem(slab + q, ns)}

    def giver(q):
        return {"dp": (xlo * nz + lax.rem(z + nz - q, nz)) * 2 + core, "slab": z}

    loads = [
        pltpu.make_async_copy(pre_hbm.at[0], pre_v, load_sem.at[0]),
        pltpu.make_async_copy(gn_hbm.at[0], gn_v, load_sem.at[1]),
    ]
    for c in loads:
        c.start()

    barrier = pltpu.get_barrier_semaphore()
    for q in range(1, ns):
        pl.semaphore_signal(barrier, inc=1, device_id=image_device(peer(q)), device_id_type=MESH)
    pl.semaphore_signal(barrier, inc=1, device_id=other_core, device_id_type=MESH)
    pl.semaphore_signal(barrier, inc=1, device_id=other_x, device_id_type=MESH)
    for q in range(1, ns):
        pl.semaphore_signal(barrier, inc=1, device_id=owner(q), device_id_type=MESH)
        pl.semaphore_signal(barrier, inc=1, device_id=giver(q), device_id_type=MESH)

    @pl.when(jnp.logical_not(own_final))
    def _():
        pl.semaphore_signal(barrier, inc=1, device_id=owner(0), device_id_type=MESH)
        pl.semaphore_signal(barrier, inc=1, device_id=giver(0), device_id_type=MESH)

    half = lax.div(slab, ns // 2)
    part = lax.rem(slab + ns // 2, ns)
    row_tap = 2 * half
    weights = [
        pltpu.make_async_copy(w_hbm.at[1], wv.at[0], w_sem.at[0]),
        pltpu.make_async_copy(w_hbm.at[row_tap], wv.at[1], w_sem.at[1]),
    ]

    def lanes(a, s):
        return pl.ds(pl.multiple_of(a * (cin // 2) + s * gran, gran), gran)

    own_x = [
        pltpu.make_async_copy(
            x_hbm.at[0, :, :, lanes(a, slab)],
            xr.at[slab, :, :, pl.ds(a * gran, gran)],
            x_loc.at[a],
        )
        for a in range(2)
    ]
    for c in own_x:
        c.start()

    for c in loads:
        c.wait()
    saved = pre_v[...].astype(F32)
    up = gn_v[...].astype(F32)

    def total(v):
        return jnp.sum(jnp.sum(v, axis=0), axis=0, keepdims=True)

    s1 = total(saved)
    centred = saved - s1 / (rows * cols)
    own_stats = [s1, total(centred * centred), total(up), total(up * centred)]
    st[slab] = jnp.concatenate(own_stats + [jnp.zeros((4, cout), F32)], axis=0)
    xf[:, side * 2 :, :] = jnp.zeros((ns * rows, pad - 2 * side, 2 * gran), BF16)
    gf[:, side * 2 :, :] = jnp.zeros((ns * rows, pad - 2 * side, cout), BF16)
    xc[...] = jnp.zeros(xc.shape, BF16)
    gc[...] = jnp.zeros(gc.shape, BF16)

    pl.semaphore_wait(barrier, (ns - 1) + 2 + 2 * ns - 2 * own_final.astype(jnp.int32))

    sends = []

    def send(src, dst, s_sem, r_sem, device):
        c = pltpu.make_async_remote_copy(
            src_ref=src, dst_ref=dst, send_sem=s_sem, recv_sem=r_sem,
            device_id=device, device_id_type=MESH,
        )
        c.start()
        sends.append(c)
        return c

    st_copies = [
        send(st.at[slab], st.at[slab], st_s.at[q], st_r.at[q], image_device(peer(q)))
        for q in range(1, ns)
    ]
    x_copies = {}
    for q in range(1, ns):
        for a in range(2):
            x_copies[q, a] = send(
                x_hbm.at[0, :, :, lanes(a, peer(q))],
                xr.at[slab, :, :, pl.ds(a * gran, gran)],
                x_s.at[q, a], x_r.at[q, a], image_device(peer(q)),
            )
    for c in weights:
        c.start()

    for c in st_copies:
        c.wait_recv()
    every = st[...]
    mean = jnp.sum(every[:, 0:1], axis=0) / cells
    m2 = jnp.zeros((1, cout), F32)
    sum_g = jnp.zeros((1, cout), F32)
    sum_gc = jnp.zeros((1, cout), F32)
    for k in range(ns):
        off = every[k, 0:1] / (rows * cols) - mean
        m2 = m2 + every[k, 1:2] + (rows * cols) * off * off
        sum_g = sum_g + every[k, 2:3]
        sum_gc = sum_gc + every[k, 3:4] + every[k, 2:3] * off
    inv_std = lax.rsqrt(m2 / cells + EPSILON)
    sum_gz = sum_gc * inv_std
    zhat = (saved - mean) * inv_std
    grad = (gain_ref[...] * inv_std) * (up - sum_g / cells - zhat * (sum_gz / cells))
    gr[slab] = grad.astype(BF16)
    g_copies = {
        q: send(gr.at[slab], gr.at[slab], g_s.at[q], g_r.at[q], image_device(peer(q)))
        for q in range(1, ns)
    }
    gb[...] = jnp.concatenate([sum_gz, sum_g, jnp.zeros((6, cout), F32)], axis=0)
    gbc_copy = send(gb, gbc, gc_s, gc_r, other_core)

    def unpack(block, full, corner, k):
        v = block[k]
        at = pl.ds(k * rows, rows)
        full[at, 0:cols, :] = v
        corner[at, 0:third, :] = v[:, cols - third :, :]

    unpack(gr, gf, gc, slab)
    for c in own_x:
        c.wait()
    unpack(xr, xf, xc, slab)

    gbc_copy.wait_recv()
    gbk[...] = gb[...] + gbc[...]
    gbx_copy = send(gbk, gbx, gl_s, gl_r, other_x)

    for q in range(1, ns):
        x_copies[q, 0].wait_recv()
        x_copies[q, 1].wait_recv()
        unpack(xr, xf, xc, source(q))
    for q in range(1, ns):
        g_copies[q].wait_recv()
        unpack(gr, gf, gc, source(q))

    gbx_copy.wait_recv()
    gbs[...] = gbk[...] + gbx[...]

    place = lax.rem(z + nz - slab, nz)

    def to_owners(src_of, dst, s_sem, r_sem, loc_sem):
        for q in range(1, ns):
            send(src_of(q), dst, s_sem.at[q], r_sem.at[place], owner(q))
        first = pltpu.make_async_remote_copy(
            src_ref=src_of(0), dst_ref=dst, send_sem=s_sem.at[0], recv_sem=r_sem.at[place],
            device_id=owner(0), device_id_type=MESH,
        )
        local = pltpu.make_async_copy(src_of(0), dst, loc_sem)

        @pl.when(own_final)
        def _():
            local.start()

        @pl.when(jnp.logical_not(own_final))
        def _():
            first.start()

        return first, local

    def from_givers(copies, dst, s_sem, r_sem):
        first, local = copies

        def arrival(idx):
            at = dst.at[lax.rem(z + idx, nz)]
            return pltpu.make_async_remote_copy(
                src_ref=at, dst_ref=at, send_sem=s_sem.at[0], recv_sem=r_sem.at[idx],
                device_id=other_core, device_id_type=MESH,
            )

        for idx in range(1, nz):
            arrival(idx).wait_recv()

        @pl.when(own_final)
        def _():
            local.wait()

        @pl.when(jnp.logical_not(own_final))
        def _():
            first.wait_send()
            arrival(0).wait_recv()

    gbf_copies = to_owners(lambda q: gbs, gbf.at[z], gf_s, gf_r, gb_loc)

    hh = ns * rows // 2

    def weight_tap(t):
        i, j = TAPS[t]
        h0, h1 = ((0, hh), (0, 2 * hh), (hh, 2 * hh))[i]
        g0, g1 = ((hh, 2 * hh), (0, 2 * hh), (0, hh))[i]
        xs = (xf[h0:h1, 0:side], xf[h0:h1], xc[h0:h1])[j]
        gs = (gc[g0:g1], gf[g0:g1], gf[g0:g1, 0:side])[j]
        n = xs.shape[0] * xs.shape[1]
        prod = lax.dot_general(
            xs.reshape(n, 2 * gran), gs.reshape(n, cout),
            (((0,), (0,)), ((), ())), preferred_element_type=F32,
        )
        dw[t] = prod.reshape(2, 2, gran // 2, cout)
        return send(
            dw.at[t, :, 1 - core], crecv.at[t], c_s.at[t], c_r.at[t], other_core
        )

    def core_stage(t, copy):
        copy.wait_recv()
        keep[t] = dw[t, xlo, core] + crecv[t, xlo]
        xsend[t] = (dw[t, 1 - xlo, core] + crecv[t, 1 - xlo]).astype(BF16)
        return send(xsend.at[t], xrecv.at[t], l_s.at[t], l_r.at[t], other_x)

    def x_stage(t, copy):
        copy.wait_recv()
        v = (keep[t] + xrecv[t].astype(F32)).reshape(ns, 8, cout)
        v = jnp.concatenate([v[:, :, : cout // 2], v[:, :, cout // 2 :]], axis=1)
        fsend[:, t] = v.astype(BF16)

    chunk = 256 if cin % 256 == 0 else cin

    def input_chunk(n, carry):
        at = pl.ds(pl.multiple_of(n * chunk, chunk), chunk)

        def prod(g, w):
            m = g.shape[0] * g.shape[1]
            return lax.dot_general(
                g.reshape(m, cout), w, (((1,), (1,)), ((), ())), preferred_element_type=F32
            ).reshape(g.shape[0], g.shape[1], chunk)

        mine, theirs = pl.ds(slab * rows, rows), pl.ds(part * rows, rows)
        mid = prod(gf[mine], wv[0, 1, at]) + prod(gf[theirs], wv[1, 1, at])
        first = prod(gc[mine], wv[0, 0, at]) + prod(gc[theirs], wv[1, 0, at])
        last = prod(gf[mine, 0:side], wv[0, 2, at]) + prod(gf[theirs, 0:side], wv[1, 2, at])
        tail = cols - third
        gin_v[:, :, at] = jnp.concatenate(
            [
                mid[:, :side] + first,
                mid[:, side:tail],
                mid[:, tail:cols] + last[:, :third],
            ],
            axis=1,
        ).astype(BF16)
        return carry

    nt = len(TAPS)
    c_copies, l_copies = {}, {}
    for step in range(nt + 1):
        if step < nt:
            c_copies[step] = weight_tap(step)
        if step >= 1:
            l_copies[step - 1] = core_stage(step - 1, c_copies[step - 1])
    for t in range(nt):
        x_stage(t, l_copies[t])
    f_copies = to_owners(
        lambda q: fsend.at[lax.rem(slab + q, ns)], frecv.at[z], f_s, f_r, f_loc
    )
    for c in weights:
        c.wait()
    lax.fori_loop(0, cin // chunk, input_chunk, 0)
    gin_copy = pltpu.make_async_copy(gin_v, gin_ref.at[0], gin_sem)
    gin_copy.start()

    from_givers(gbf_copies, gbf, gf_s, gf_r)
    both = jnp.sum(gbf[...], axis=0)
    gg_ref[...] = both[0:1]
    bg_ref[...] = both[1:2]
    from_givers(f_copies, frecv, f_s, f_r)
    acc = frecv[0].astype(F32)
    for k in range(1, nz):
        acc = acc + frecv[k].astype(F32)
    for t, (i, j) in enumerate(TAPS):
        wg_ref[i, j] = jnp.concatenate([acc[t, :8], acc[t, 8:]], axis=1)
    for c in sends:
        c.wait_send()
    gin_copy.wait()


def per_device(inputs, weight, pre_norm, grad_norm, norm_gain):
    ns = lax.axis_size("slab")
    nz = lax.axis_size("dp") // 4
    _, rows, cols, cin = inputs.shape
    cout = pre_norm.shape[3]
    sizes = (ns, nz, rows, cols, cin, cout)
    block = 2 * (cin // (2 * ns))
    height = ns * rows
    pad, side = 48, 16
    nt = len(TAPS)
    dma = pltpu.SemaphoreType.DMA
    any_spec = pl.BlockSpec(memory_space=pl.ANY)
    vmem_spec = pl.BlockSpec(memory_space=pltpu.VMEM)
    scratch = [
        pltpu.VMEM((rows, cols, cout), BF16),
        pltpu.VMEM((rows, cols, cout), BF16),
        pltpu.VMEM((ns, 8, cout), F32),
        pltpu.VMEM((ns, rows, cols, block), BF16),
        pltpu.VMEM((ns, rows, cols, cout), BF16),
        pltpu.VMEM((height, pad, block), BF16),
        pltpu.VMEM((height, side, block), BF16),
        pltpu.VMEM((height, pad, cout), BF16),
        pltpu.VMEM((height, side, cout), BF16),
        pltpu.VMEM((2, 3, cin, cout), BF16),
        pltpu.VMEM((rows, cols, cin), BF16),
        pltpu.VMEM((nt, 2, 2, block // 4, cout), F32),
        pltpu.VMEM((nt, 2, block // 4, cout), F32),
        pltpu.VMEM((nt, block // 4, cout), F32),
        pltpu.VMEM((nt, block // 4, cout), BF16),
        pltpu.VMEM((nt, block // 4, cout), BF16),
        pltpu.VMEM((ns, nt, 16, cout // 2), BF16),
        pltpu.VMEM((nz, nt, 16, cout // 2), BF16),
        pltpu.VMEM((8, cout), F32),
        pltpu.VMEM((8, cout), F32),
        pltpu.VMEM((8, cout), F32),
        pltpu.VMEM((8, cout), F32),
        pltpu.VMEM((8, cout), F32),
        pltpu.VMEM((nz, 8, cout), F32),
        dma((2,)), dma((2,)), dma((2,)), dma, dma, dma,
        dma((ns,)), dma((ns,)), dma((ns, 2)), dma((ns, 2)), dma((ns,)), dma((ns,)),
        dma((nt,)), dma((nt,)), dma((nt,)), dma((nt,)), dma((ns,)), dma((ns,)),
        dma, dma, dma, dma, dma((ns,)), dma((ns,)),
    ]
    gin, wg, gg, bg = pl.pallas_call(
        functools.partial(kernel, sizes),
        out_shape=(
            jax.ShapeDtypeStruct(inputs.shape, BF16),
            jax.ShapeDtypeStruct((3, 3, cin // (ns * nz * 4), cout), F32),
            jax.ShapeDtypeStruct((1, cout), F32),
            jax.ShapeDtypeStruct((1, cout), F32),
        ),
        in_specs=[any_spec, any_spec, any_spec, any_spec, vmem_spec],
        out_specs=(any_spec, vmem_spec, vmem_spec, vmem_spec),
        scratch_shapes=scratch,
        compiler_params=pltpu.CompilerParams(
            collective_id=0, has_side_effects=True, vmem_limit_bytes=56 * 1024 * 1024
        ),
    )(inputs, weight, pre_norm, grad_norm, norm_gain.reshape(1, cout))
    return gin, wg, gg.reshape(cout), bg.reshape(cout)


def solution(mesh):
    placed = (
        P("dp", "slab", None, None),
        P(),
        P("dp", "slab", None, None),
        P("dp", "slab", None, None),
        P(),
    )
    return jax.shard_map(
        per_device,
        mesh=mesh,
        in_specs=placed,
        out_specs=(P("dp", "slab", None, None), P(None, None, ("dp", "slab"), None), P(), P()),
        check_vma=False,
    )
```

```python
import functools

import jax
import jax.numpy as jnp
from jax import lax
from jax.experimental import pallas as pl
from jax.experimental.pallas import tpu as pltpu
from jax.sharding import PartitionSpec as P

MESH = pl.DeviceIdType.MESH
F32 = jnp.float32
BF16 = jnp.bfloat16
EPSILON = 1e-05
TAPS = ((1, 1), (0, 1), (2, 1), (1, 0), (1, 2), (0, 0), (0, 2), (2, 0), (2, 2))
GROUPS = ((0, 1, 2), (3, 4, 5), (6, 7, 8))


def kernel(
    sizes,
    x_hbm, w_hbm, pre_hbm, gn_hbm, gain_ref,
    gin_ref, small_ref,
    pre_v, gn_v, st, xr, gr, xf, xc, gf, gc, wv, gin_v,
    dw, crecv, ssend, srecv, zsend, zrecv,
    gb, gbc, gbk, gbx, gbz,
    load_sem, w_sem, x_loc, gin_sem,
    st_s, st_r, x_s, x_r, g_s, g_r, c_s, c_r, s_s, s_r, z_s, z_r,
    gc_s, gc_r, gl_s, gl_r, gz_s, gz_r,
):
    ns, nz, rows, cols, cin, cout = sizes
    gran = cin // (2 * ns)
    pad = xf.shape[1]
    side = xc.shape[1]
    third = cols // 3
    cells = rows * cols * ns
    slab = lax.axis_index("slab")
    dp = lax.axis_index("dp")
    core = lax.rem(dp, 2)
    z = lax.rem(lax.div(dp, 2), nz)
    xlo = lax.div(dp, 2 * nz)
    other_core = {"dp": dp + 1 - 2 * core, "slab": slab}
    other_x = {"dp": dp + (1 - 2 * xlo) * (2 * nz), "slab": slab}
    nt = len(TAPS)

    def peer(q):
        return lax.rem(slab + q, ns)

    def source(q):
        return lax.rem(slab + ns - q, ns)

    def image_device(q):
        return {"dp": dp, "slab": peer(q)}

    def z_peer(q):
        return lax.rem(z + q, nz)

    def z_device(q):
        return {"dp": (xlo * nz + z_peer(q)) * 2 + core, "slab": slab}

    def pair_device(e, q):
        return {"dp": (xlo + e * (1 - 2 * xlo)) * (2 * nz) + lax.rem(dp, 2 * nz), "slab": peer(q)}

    pair_steps = [(e, q) for e in range(2) for q in range(ns) if e or q]

    loads = [
        pltpu.make_async_copy(pre_hbm.at[0], pre_v, load_sem.at[0]),
        pltpu.make_async_copy(gn_hbm.at[0], gn_v, load_sem.at[1]),
    ]
    for c in loads:
        c.start()

    barrier = pltpu.get_barrier_semaphore()
    friends = [pair_device(e, q) for e, q in pair_steps] + [other_core]
    friends += [z_device(q) for q in range(1, nz)]
    for friend in friends:
        pl.semaphore_signal(barrier, inc=1, device_id=friend, device_id_type=MESH)

    half = lax.div(slab, ns // 2)
    part = lax.rem(slab + ns // 2, ns)
    row_tap = 2 * half
    weights = [
        pltpu.make_async_copy(w_hbm.at[1], wv.at[0], w_sem.at[0]),
        pltpu.make_async_copy(w_hbm.at[row_tap], wv.at[1], w_sem.at[1]),
    ]

    def lanes(a, s):
        return pl.ds(pl.multiple_of(a * (cin // 2) + s * gran, gran), gran)

    own_x = [
        pltpu.make_async_copy(
            x_hbm.at[0, :, :, lanes(a, slab)],
            xr.at[slab, :, :, pl.ds(a * gran, gran)],
            x_loc.at[a],
        )
        for a in range(2)
    ]
    for c in own_x:
        c.start()

    for c in loads:
        c.wait()
    saved = pre_v[...].astype(F32)
    up = gn_v[...].astype(F32)

    def total(v):
        return jnp.sum(jnp.sum(v, axis=0), axis=0, keepdims=True)

    s1 = total(saved)
    centred = saved - s1 / (rows * cols)
    own_stats = [s1, total(centred * centred), total(up), total(up * centred)]
    st[slab] = jnp.concatenate(own_stats + [jnp.zeros((4, cout), F32)], axis=0)
    xf[:, side * 2 :, :] = jnp.zeros((ns * rows, pad - 2 * side, 2 * gran), BF16)
    gf[:, side * 2 :, :] = jnp.zeros((ns * rows, pad - 2 * side, cout), BF16)
    xc[...] = jnp.zeros(xc.shape, BF16)
    gc[...] = jnp.zeros(gc.shape, BF16)

    pl.semaphore_wait(barrier, len(friends))

    sends = []

    def send(src, dst, s_sem, r_sem, device):
        c = pltpu.make_async_remote_copy(
            src_ref=src, dst_ref=dst, send_sem=s_sem, recv_sem=r_sem,
            device_id=device, device_id_type=MESH,
        )
        c.start()
        sends.append(c)
        return c

    st_copies = [
        send(st.at[slab], st.at[slab], st_s.at[q], st_r.at[q], image_device(q))
        for q in range(1, ns)
    ]
    x_copies = {}
    for q in range(1, ns):
        for a in range(2):
            x_copies[q, a] = send(
                x_hbm.at[0, :, :, lanes(a, peer(q))],
                xr.at[slab, :, :, pl.ds(a * gran, gran)],
                x_s.at[q, a], x_r.at[q, a], image_device(q),
            )
    for c in weights:
        c.start()

    for c in st_copies:
        c.wait_recv()
    every = st[...]
    mean = jnp.sum(every[:, 0:1], axis=0) / cells
    m2 = jnp.zeros((1, cout), F32)
    sum_g = jnp.zeros((1, cout), F32)
    sum_gc = jnp.zeros((1, cout), F32)
    for k in range(ns):
        off = every[k, 0:1] / (rows * cols) - mean
        m2 = m2 + every[k, 1:2] + (rows * cols) * off * off
        sum_g = sum_g + every[k, 2:3]
        sum_gc = sum_gc + every[k, 3:4] + every[k, 2:3] * off
    inv_std = lax.rsqrt(m2 / cells + EPSILON)
    sum_gz = sum_gc * inv_std
    zhat = (saved - mean) * inv_std
    grad = (gain_ref[...] * inv_std) * (up - sum_g / cells - zhat * (sum_gz / cells))
    gr[slab] = grad.astype(BF16)
    g_order = [ns // 2] + [q for q in range(1, ns) if q != ns // 2]
    g_copies = {
        q: send(gr.at[slab], gr.at[slab], g_s.at[q], g_r.at[q], image_device(q)) for q in g_order
    }
    gb[...] = jnp.concatenate([sum_gz, sum_g, jnp.zeros((6, cout), F32)], axis=0)
    gbc_copy = send(gb, gbc, gc_s, gc_r, other_core)

    def unpack(block, full, corner, k):
        v = block[k]
        at = pl.ds(k * rows, rows)
        full[at, 0:cols, :] = v
        corner[at, 0:third, :] = v[:, cols - third :, :]

    unpack(gr, gf, gc, slab)
    for c in own_x:
        c.wait()
    unpack(xr, xf, xc, slab)

    gbc_copy.wait_recv()
    gbk[...] = gb[...] + gbc[...]
    gbx_copy = send(gbk, gbx, gl_s, gl_r, other_x)

    for q in range(1, ns):
        x_copies[q, 0].wait_recv()
        x_copies[q, 1].wait_recv()
        unpack(xr, xf, xc, source(q))
    gbx_copy.wait_recv()
    gbz[z] = gbk[...] + gbx[...]
    gbz_copies = [
        send(gbz.at[z], gbz.at[z], gz_s.at[q], gz_r.at[q], z_device(q)) for q in range(1, nz)
    ]

    hh = ns * rows // 2

    def weight_tap(t):
        i, j = TAPS[t]
        h0, h1 = ((0, hh), (0, 2 * hh), (hh, 2 * hh))[i]
        g0, g1 = ((hh, 2 * hh), (0, 2 * hh), (0, hh))[i]
        xs = (xf[h0:h1, 0:side], xf[h0:h1], xc[h0:h1])[j]
        gs = (gc[g0:g1], gf[g0:g1], gf[g0:g1, 0:side])[j]
        n = xs.shape[0] * xs.shape[1]
        prod = lax.dot_general(
            xs.reshape(n, 2 * gran), gs.reshape(n, cout),
            (((0,), (0,)), ((), ())), preferred_element_type=F32,
        )
        dw[t] = prod.reshape(2, 2, gran // 2, cout)
        return send(
            dw.at[t, :, 1 - core], crecv.at[t], c_s.at[t], c_r.at[t], other_core
        )

    def core_stage(t, copy):
        copy.wait_recv()
        v = (dw[t, :, core] + crecv[t]).reshape(2, ns, 8, cout)
        v = jnp.concatenate([v[:, :, :, : cout // 2], v[:, :, :, cout // 2 :]], axis=2)
        ssend[:, :, t] = v.astype(BF16)

    def pair_send(g):
        at = pl.ds(GROUPS[g][0], len(GROUPS[g]))
        copies = []
        for e, q in pair_steps:
            to_x = xlo + e * (1 - 2 * xlo)
            copies.append(
                send(
                    ssend.at[to_x, peer(q), at], srecv.at[xlo, slab, at],
                    s_s.at[g, e, q], s_r.at[g, e, q], pair_device(e, q),
                )
            )
        srecv[xlo, slab, at] = ssend[xlo, slab, at]
        return copies

    def z_send(g, copies):
        for c in copies:
            c.wait_recv()
        at = pl.ds(GROUPS[g][0], len(GROUPS[g]))
        zsend[:, at] = (srecv[0, :, at].astype(F32) + srecv[1, :, at].astype(F32)).astype(BF16)
        out = [
            send(zsend.at[z_peer(q), at], zrecv.at[z, at], z_s.at[g, q], z_r.at[g, q], z_device(q))
            for q in range(1, nz)
        ]
        zrecv[z, at] = zsend[z, at]
        return out

    chunk = 256 if cin % 256 == 0 else cin

    def input_chunk(n, carry):
        at = pl.ds(pl.multiple_of(n * chunk, chunk), chunk)

        def prod(g, w):
            m = g.shape[0] * g.shape[1]
            return lax.dot_general(
                g.reshape(m, cout), w, (((1,), (1,)), ((), ())), preferred_element_type=F32
            ).reshape(g.shape[0], g.shape[1], chunk)

        mine, theirs = pl.ds(slab * rows, rows), pl.ds(part * rows, rows)
        mid = prod(gf[mine], wv[0, 1, at]) + prod(gf[theirs], wv[1, 1, at])
        first = prod(gc[mine], wv[0, 0, at]) + prod(gc[theirs], wv[1, 0, at])
        last = prod(gf[mine, 0:side], wv[0, 2, at]) + prod(gf[theirs, 0:side], wv[1, 2, at])
        tail = cols - third
        gin_v[:, :, at] = jnp.concatenate(
            [
                mid[:, :side] + first,
                mid[:, side:tail],
                mid[:, tail:cols] + last[:, :third],
            ],
            axis=1,
        ).astype(BF16)
        return carry

    for q in g_order[:1]:
        g_copies[q].wait_recv()
        unpack(gr, gf, gc, source(q))
    for c in weights:
        c.wait()
    lax.fori_loop(0, cin // chunk, input_chunk, 0)
    gin_copy = pltpu.make_async_copy(gin_v, gin_ref.at[0], gin_sem)
    gin_copy.start()
    for q in g_order[1:]:
        g_copies[q].wait_recv()
        unpack(gr, gf, gc, source(q))

    ng = len(GROUPS)
    c_copies, s_copies, z_copies = {}, {}, {}
    for step in range(ng + 2):
        if step < ng:
            for t in GROUPS[step]:
                c_copies[t] = weight_tap(t)
        if 1 <= step <= ng:
            for t in GROUPS[step - 1]:
                core_stage(t, c_copies[t])
            s_copies[step - 1] = pair_send(step - 1)
        if step >= 2:
            z_copies[step - 2] = z_send(step - 2, s_copies[step - 2])

    for c in gbz_copies:
        c.wait_recv()
    small_ref[nt] = jnp.sum(gbz[...], axis=0)
    for g in range(ng):
        for c in z_copies[g]:
            c.wait_recv()
        at = pl.ds(GROUPS[g][0], len(GROUPS[g]))
        acc = zrecv[0, at].astype(F32)
        for k in range(1, nz):
            acc = acc + zrecv[k, at].astype(F32)
        small_ref[at] = jnp.concatenate([acc[:, :8], acc[:, 8:]], axis=2)
    for c in sends:
        c.wait_send()
    gin_copy.wait()


def results(gin_in, small_in, gin_ref, wg_ref, gg_ref, bg_ref, sem):
    copy = pltpu.make_async_copy(gin_in, gin_ref, sem)
    copy.start()
    for t, (i, j) in enumerate(TAPS):
        wg_ref[i, j] = small_in[t]
    gg_ref[...] = small_in[len(TAPS), 0:1]
    bg_ref[...] = small_in[len(TAPS), 1:2]
    copy.wait()


def per_device(inputs, weight, pre_norm, grad_norm, norm_gain):
    ns = lax.axis_size("slab")
    nz = lax.axis_size("dp") // 4
    _, rows, cols, cin = inputs.shape
    cout = pre_norm.shape[3]
    sizes = (ns, nz, rows, cols, cin, cout)
    block = 2 * (cin // (2 * ns))
    height = ns * rows
    pad, side = 48, 16
    nt, ng = len(TAPS), len(GROUPS)
    dma = pltpu.SemaphoreType.DMA
    any_spec = pl.BlockSpec(memory_space=pl.ANY)
    vmem_spec = pl.BlockSpec(memory_space=pltpu.VMEM)
    scratch = [
        pltpu.VMEM((rows, cols, cout), BF16),
        pltpu.VMEM((rows, cols, cout), BF16),
        pltpu.VMEM((ns, 8, cout), F32),
        pltpu.VMEM((ns, rows, cols, block), BF16),
        pltpu.VMEM((ns, rows, cols, cout), BF16),
        pltpu.VMEM((height, pad, block), BF16),
        pltpu.VMEM((height, side, block), BF16),
        pltpu.VMEM((height, pad, cout), BF16),
        pltpu.VMEM((height, side, cout), BF16),
        pltpu.VMEM((2, 3, cin, cout), BF16),
        pltpu.VMEM((rows, cols, cin), BF16),
        pltpu.VMEM((nt, 2, 2, block // 4, cout), F32),
        pltpu.VMEM((nt, 2, block // 4, cout), F32),
        pltpu.VMEM((2, ns, nt, 16, cout // 2), BF16),
        pltpu.VMEM((2, ns, nt, 16, cout // 2), BF16),
        pltpu.VMEM((nz, nt, 16, cout // 2), BF16),
        pltpu.VMEM((nz, nt, 16, cout // 2), BF16),
        pltpu.VMEM((8, cout), F32),
        pltpu.VMEM((8, cout), F32),
        pltpu.VMEM((8, cout), F32),
        pltpu.VMEM((8, cout), F32),
        pltpu.VMEM((nz, 8, cout), F32),
        dma((2,)), dma((2,)), dma((2,)), dma,
        dma((ns,)), dma((ns,)), dma((ns, 2)), dma((ns, 2)), dma((ns,)), dma((ns,)),
        dma((nt,)), dma((nt,)), dma((ng, 2, ns)), dma((ng, 2, ns)), dma((ng, nz)), dma((ng, nz)),
        dma, dma, dma, dma, dma((nz,)), dma((nz,)),
    ]
    gin, small = pl.pallas_call(
        functools.partial(kernel, sizes),
        out_shape=(
            jax.ShapeDtypeStruct(inputs.shape, BF16),
            jax.ShapeDtypeStruct((nt + 1, 8, cout), F32),
        ),
        in_specs=[any_spec, any_spec, any_spec, any_spec, vmem_spec],
        out_specs=(any_spec, vmem_spec),
        scratch_shapes=scratch,
        compiler_params=pltpu.CompilerParams(
            collective_id=0, has_side_effects=True, vmem_limit_bytes=56 * 1024 * 1024
        ),
    )(inputs, weight, pre_norm, grad_norm, norm_gain.reshape(1, cout))
    gin, wg, gg, bg = pl.pallas_call(
        results,
        out_shape=(
            jax.ShapeDtypeStruct(inputs.shape, BF16),
            jax.ShapeDtypeStruct((3, 3, 8, cout), F32),
            jax.ShapeDtypeStruct((1, cout), F32),
            jax.ShapeDtypeStruct((1, cout), F32),
        ),
        in_specs=[any_spec, vmem_spec],
        out_specs=(any_spec, vmem_spec, vmem_spec, vmem_spec),
        scratch_shapes=[dma],
    )(gin, small)
    return gin, wg, gg.reshape(cout), bg.reshape(cout)


def solution(mesh):
    placed = (
        P("dp", "slab", None, None),
        P(),
        P("dp", "slab", None, None),
        P("dp", "slab", None, None),
        P(),
    )
    return jax.shard_map(
        per_device,
        mesh=mesh,
        in_specs=placed,
        out_specs=(P("dp", "slab", None, None), P(None, None, ("dp", "slab"), None), P(), P()),
        check_vma=False,
    )
```

```python
import functools

import jax
import jax.numpy as jnp
from jax import lax
from jax.experimental import pallas as pl
from jax.experimental.pallas import tpu as pltpu
from jax.sharding import PartitionSpec as P

MESH = pl.DeviceIdType.MESH
F32 = jnp.float32
BF16 = jnp.bfloat16
EPSILON = 1e-05
TAPS = ((1, 1), (0, 1), (2, 1), (1, 0), (1, 2), (0, 0), (0, 2), (2, 0), (2, 2))
GROUPS = ((0, 1, 2), (3, 4, 5), (6, 7, 8))


def kernel(
    sizes,
    x_hbm, w_hbm, pre_hbm, gn_hbm, gain_ref,
    gin_ref, small_ref,
    pre_v, gn_v, st, xr, gr, xf, xc, gf, gc, wv, gin_v,
    dw, crecv, ssend, srecv, zsend, zrecv,
    gb, gbc, gbk, gbx, gbz,
    load_sem, w_sem, x_loc, gin_sem,
    st_s, st_r, x_s, x_r, g_s, g_r, c_s, c_r, s_s, s_r, z_s, z_r,
    gc_s, gc_r, gl_s, gl_r, gz_s, gz_r,
):
    ns, nz, rows, cols, cin, cout = sizes
    gran = cin // (2 * ns)
    pad = xf.shape[1]
    side = xc.shape[1]
    third = cols // 3
    cells = rows * cols * ns
    slab = lax.axis_index("slab")
    dp = lax.axis_index("dp")
    core = lax.rem(dp, 2)
    z = lax.rem(lax.div(dp, 2), nz)
    xlo = lax.div(dp, 2 * nz)
    other_core = {"dp": dp + 1 - 2 * core, "slab": slab}
    other_x = {"dp": dp + (1 - 2 * xlo) * (2 * nz), "slab": slab}
    nt = len(TAPS)

    def peer(q):
        return lax.rem(slab + q, ns)

    def source(q):
        return lax.rem(slab + ns - q, ns)

    def image_device(q):
        return {"dp": dp, "slab": peer(q)}

    def z_peer(q):
        return lax.rem(z + q, nz)

    def z_device(q):
        return {"dp": (xlo * nz + z_peer(q)) * 2 + core, "slab": slab}

    def pair_device(e, q):
        return {"dp": (xlo + e * (1 - 2 * xlo)) * (2 * nz) + lax.rem(dp, 2 * nz), "slab": peer(q)}

    pair_steps = [(e, q) for e in range(2) for q in range(ns) if e or q]

    loads = [
        pltpu.make_async_copy(pre_hbm.at[0], pre_v, load_sem.at[0]),
        pltpu.make_async_copy(gn_hbm.at[0], gn_v, load_sem.at[1]),
    ]
    for c in loads:
        c.start()

    barrier = pltpu.get_barrier_semaphore()
    friends = [pair_device(e, q) for e, q in pair_steps] + [other_core]
    friends += [z_device(q) for q in range(1, nz)]
    for friend in friends:
        pl.semaphore_signal(barrier, inc=1, device_id=friend, device_id_type=MESH)

    half = lax.div(slab, ns // 2)
    part = lax.rem(slab + ns // 2, ns)
    row_tap = 2 * half
    weights = [
        pltpu.make_async_copy(w_hbm.at[1], wv.at[0], w_sem.at[0]),
        pltpu.make_async_copy(w_hbm.at[row_tap], wv.at[1], w_sem.at[1]),
    ]

    def lanes(a, s):
        return pl.ds(pl.multiple_of(a * (cin // 2) + s * gran, gran), gran)

    own_x = [
        pltpu.make_async_copy(
            x_hbm.at[0, :, :, lanes(a, slab)],
            xr.at[slab, :, :, pl.ds(a * gran, gran)],
            x_loc.at[a],
        )
        for a in range(2)
    ]
    for c in own_x:
        c.start()

    for c in loads:
        c.wait()
    saved = pre_v[...].astype(F32)
    up = gn_v[...].astype(F32)

    def total(v):
        return jnp.sum(jnp.sum(v, axis=0), axis=0, keepdims=True)

    s1 = total(saved)
    centred = saved - s1 / (rows * cols)
    own_stats = [s1, total(centred * centred), total(up), total(up * centred)]
    st[slab] = jnp.concatenate(own_stats + [jnp.zeros((4, cout), F32)], axis=0)
    xf[:, side * 2 :, :] = jnp.zeros((ns * rows, pad - 2 * side, 2 * gran), BF16)
    gf[:, side * 2 :, :] = jnp.zeros((ns * rows, pad - 2 * side, cout), BF16)
    xc[...] = jnp.zeros(xc.shape, BF16)
    gc[...] = jnp.zeros(gc.shape, BF16)

    pl.semaphore_wait(barrier, len(friends))

    sends = []

    def send(src, dst, s_sem, r_sem, device):
        c = pltpu.make_async_remote_copy(
            src_ref=src, dst_ref=dst, send_sem=s_sem, recv_sem=r_sem,
            device_id=device, device_id_type=MESH,
        )
        c.start()
        sends.append(c)
        return c

    st_copies = [
        send(st.at[slab], st.at[slab], st_s.at[q], st_r.at[q], image_device(q))
        for q in range(1, ns)
    ]
    x_copies = {}
    for q in range(1, ns):
        for a in range(2):
            x_copies[q, a] = send(
                x_hbm.at[0, :, :, lanes(a, peer(q))],
                xr.at[slab, :, :, pl.ds(a * gran, gran)],
                x_s.at[q, a], x_r.at[q, a], image_device(q),
            )
    for c in weights:
        c.start()

    for c in st_copies:
        c.wait_recv()
    every = st[...]
    mean = jnp.sum(every[:, 0:1], axis=0) / cells
    m2 = jnp.zeros((1, cout), F32)
    sum_g = jnp.zeros((1, cout), F32)
    sum_gc = jnp.zeros((1, cout), F32)
    for k in range(ns):
        off = every[k, 0:1] / (rows * cols) - mean
        m2 = m2 + every[k, 1:2] + (rows * cols) * off * off
        sum_g = sum_g + every[k, 2:3]
        sum_gc = sum_gc + every[k, 3:4] + every[k, 2:3] * off
    inv_std = lax.rsqrt(m2 / cells + EPSILON)
    sum_gz = sum_gc * inv_std
    zhat = (saved - mean) * inv_std
    grad = (gain_ref[...] * inv_std) * (up - sum_g / cells - zhat * (sum_gz / cells))
    gr[slab] = grad.astype(BF16)
    g_order = [ns // 2] + [q for q in range(1, ns) if q != ns // 2]
    g_copies = {
        q: send(gr.at[slab], gr.at[slab], g_s.at[q], g_r.at[q], image_device(q)) for q in g_order
    }
    gb[...] = jnp.concatenate([sum_gz, sum_g, jnp.zeros((6, cout), F32)], axis=0)
    gbc_copy = send(gb, gbc, gc_s, gc_r, other_core)

    def unpack(block, full, corner, k):
        v = block[k]
        at = pl.ds(k * rows, rows)
        full[at, 0:cols, :] = v
        corner[at, 0:third, :] = v[:, cols - third :, :]

    unpack(gr, gf, gc, slab)
    for c in own_x:
        c.wait()
    unpack(xr, xf, xc, slab)

    gbc_copy.wait_recv()
    gbk[...] = gb[...] + gbc[...]
    gbx_copy = send(gbk, gbx, gl_s, gl_r, other_x)

    for q in range(1, ns):
        x_copies[q, 0].wait_recv()
        x_copies[q, 1].wait_recv()
        unpack(xr, xf, xc, source(q))
    gbx_copy.wait_recv()
    gbz[z] = gbk[...] + gbx[...]
    gbz_copies = [
        send(gbz.at[z], gbz.at[z], gz_s.at[q], gz_r.at[q], z_device(q)) for q in range(1, nz)
    ]

    hh = ns * rows // 2

    def weight_tap(t):
        i, j = TAPS[t]
        h0, h1 = ((0, hh), (0, 2 * hh), (hh, 2 * hh))[i]
        g0, g1 = ((hh, 2 * hh), (0, 2 * hh), (0, hh))[i]
        xs = (xf[h0:h1, 0:side], xf[h0:h1], xc[h0:h1])[j]
        gs = (gc[g0:g1], gf[g0:g1], gf[g0:g1, 0:side])[j]
        n = xs.shape[0] * xs.shape[1]
        prod = lax.dot_general(
            xs.reshape(n, 2 * gran), gs.reshape(n, cout),
            (((0,), (0,)), ((), ())), preferred_element_type=F32,
        )
        dw[t] = prod.reshape(2, 2, gran // 2, cout)
        return send(
            dw.at[t, :, 1 - core], crecv.at[t], c_s.at[t], c_r.at[t], other_core
        )

    def core_stage(t, copy):
        copy.wait_recv()
        v = (dw[t, :, core] + crecv[t]).reshape(2, ns, 8, cout)
        v = jnp.concatenate([v[:, :, :, : cout // 2], v[:, :, :, cout // 2 :]], axis=2)
        ssend[:, :, t] = v.astype(BF16)

    def pair_send(g):
        at = pl.ds(GROUPS[g][0], len(GROUPS[g]))
        copies = []
        for e, q in pair_steps:
            to_x = xlo + e * (1 - 2 * xlo)
            copies.append(
                send(
                    ssend.at[to_x, peer(q), at], srecv.at[xlo, slab, at],
                    s_s.at[g, e, q], s_r.at[g, e, q], pair_device(e, q),
                )
            )
        srecv[xlo, slab, at] = ssend[xlo, slab, at]
        return copies

    def z_send(g, copies):
        for c in copies:
            c.wait_recv()
        at = pl.ds(GROUPS[g][0], len(GROUPS[g]))
        zsend[:, at] = (srecv[0, :, at].astype(F32) + srecv[1, :, at].astype(F32)).astype(BF16)
        out = [
            send(zsend.at[z_peer(q), at], zrecv.at[z, at], z_s.at[g, q], z_r.at[g, q], z_device(q))
            for q in range(1, nz)
        ]
        zrecv[z, at] = zsend[z, at]
        return out

    chunk = 256 if cin % 256 == 0 else cin

    def input_chunk(n, carry):
        at = pl.ds(pl.multiple_of(n * chunk, chunk), chunk)

        def prod(g, w):
            m = g.shape[0] * g.shape[1]
            return lax.dot_general(
                g.reshape(m, cout), w, (((1,), (1,)), ((), ())), preferred_element_type=F32
            ).reshape(g.shape[0], g.shape[1], chunk)

        mine, theirs = pl.ds(slab * rows, rows), pl.ds(part * rows, rows)
        mid = prod(gf[mine], wv[0, 1, at]) + prod(gf[theirs], wv[1, 1, at])
        first = prod(gc[mine], wv[0, 0, at]) + prod(gc[theirs], wv[1, 0, at])
        last = prod(gf[mine, 0:side], wv[0, 2, at]) + prod(gf[theirs, 0:side], wv[1, 2, at])
        tail = cols - third
        gin_v[:, :, at] = jnp.concatenate(
            [
                mid[:, :side] + first,
                mid[:, side:tail],
                mid[:, tail:cols] + last[:, :third],
            ],
            axis=1,
        ).astype(BF16)
        return carry

    for q in g_order[:1]:
        g_copies[q].wait_recv()
        unpack(gr, gf, gc, source(q))
    for c in weights:
        c.wait()
    lax.fori_loop(0, cin // chunk, input_chunk, 0)
    gin_copy = pltpu.make_async_copy(gin_v, gin_ref.at[0], gin_sem)
    gin_copy.start()
    for q in g_order[1:]:
        g_copies[q].wait_recv()
        unpack(gr, gf, gc, source(q))

    ng = len(GROUPS)
    c_copies, s_copies, z_copies = {}, {}, {}
    for step in range(ng + 2):
        if step < ng:
            for t in GROUPS[step]:
                c_copies[t] = weight_tap(t)
        if 1 <= step <= ng:
            for t in GROUPS[step - 1]:
                core_stage(t, c_copies[t])
            s_copies[step - 1] = pair_send(step - 1)
        if step >= 2:
            z_copies[step - 2] = z_send(step - 2, s_copies[step - 2])

    for c in gbz_copies:
        c.wait_recv()
    small_ref[nt] = jnp.sum(gbz[...], axis=0)
    for g in range(ng):
        for c in z_copies[g]:
            c.wait_recv()
        at = pl.ds(GROUPS[g][0], len(GROUPS[g]))
        acc = zrecv[0, at].astype(F32)
        for k in range(1, nz):
            acc = acc + zrecv[k, at].astype(F32)
        small_ref[at] = jnp.concatenate([acc[:, :8], acc[:, 8:]], axis=2)
    for c in sends:
        c.wait_send()
    gin_copy.wait()


def results(gin_in, small_in, gin_ref, wg_ref, gg_ref, bg_ref, held, in_sem, out_sem):
    rows = held.shape[0]
    into = [
        pltpu.make_async_copy(gin_in.at[0, r], held.at[r], in_sem.at[r]) for r in range(rows)
    ]
    out = [
        pltpu.make_async_copy(held.at[r], gin_ref.at[0, r], out_sem.at[r]) for r in range(rows)
    ]
    for c in into:
        c.start()
    for t, (i, j) in enumerate(TAPS):
        wg_ref[i, j] = small_in[t]
    gg_ref[...] = small_in[len(TAPS), 0:1]
    bg_ref[...] = small_in[len(TAPS), 1:2]
    for r in range(rows):
        into[r].wait()
        out[r].start()
    for c in out:
        c.wait()


def per_device(inputs, weight, pre_norm, grad_norm, norm_gain):
    ns = lax.axis_size("slab")
    nz = lax.axis_size("dp") // 4
    _, rows, cols, cin = inputs.shape
    cout = pre_norm.shape[3]
    sizes = (ns, nz, rows, cols, cin, cout)
    block = 2 * (cin // (2 * ns))
    height = ns * rows
    pad, side = 48, 16
    nt, ng = len(TAPS), len(GROUPS)
    dma = pltpu.SemaphoreType.DMA
    any_spec = pl.BlockSpec(memory_space=pl.ANY)
    vmem_spec = pl.BlockSpec(memory_space=pltpu.VMEM)
    scratch = [
        pltpu.VMEM((rows, cols, cout), BF16),
        pltpu.VMEM((rows, cols, cout), BF16),
        pltpu.VMEM((ns, 8, cout), F32),
        pltpu.VMEM((ns, rows, cols, block), BF16),
        pltpu.VMEM((ns, rows, cols, cout), BF16),
        pltpu.VMEM((height, pad, block), BF16),
        pltpu.VMEM((height, side, block), BF16),
        pltpu.VMEM((height, pad, cout), BF16),
        pltpu.VMEM((height, side, cout), BF16),
        pltpu.VMEM((2, 3, cin, cout), BF16),
        pltpu.VMEM((rows, cols, cin), BF16),
        pltpu.VMEM((nt, 2, 2, block // 4, cout), F32),
        pltpu.VMEM((nt, 2, block // 4, cout), F32),
        pltpu.VMEM((2, ns, nt, 16, cout // 2), BF16),
        pltpu.VMEM((2, ns, nt, 16, cout // 2), BF16),
        pltpu.VMEM((nz, nt, 16, cout // 2), BF16),
        pltpu.VMEM((nz, nt, 16, cout // 2), BF16),
        pltpu.VMEM((8, cout), F32),
        pltpu.VMEM((8, cout), F32),
        pltpu.VMEM((8, cout), F32),
        pltpu.VMEM((8, cout), F32),
        pltpu.VMEM((nz, 8, cout), F32),
        dma((2,)), dma((2,)), dma((2,)), dma,
        dma((ns,)), dma((ns,)), dma((ns, 2)), dma((ns, 2)), dma((ns,)), dma((ns,)),
        dma((nt,)), dma((nt,)), dma((ng, 2, ns)), dma((ng, 2, ns)), dma((ng, nz)), dma((ng, nz)),
        dma, dma, dma, dma, dma((nz,)), dma((nz,)),
    ]
    gin, small = pl.pallas_call(
        functools.partial(kernel, sizes),
        out_shape=(
            jax.ShapeDtypeStruct(inputs.shape, BF16),
            jax.ShapeDtypeStruct((nt + 1, 8, cout), F32),
        ),
        in_specs=[any_spec, any_spec, any_spec, any_spec, vmem_spec],
        out_specs=(any_spec, vmem_spec),
        scratch_shapes=scratch,
        compiler_params=pltpu.CompilerParams(
            collective_id=0, has_side_effects=True, vmem_limit_bytes=56 * 1024 * 1024
        ),
    )(inputs, weight, pre_norm, grad_norm, norm_gain.reshape(1, cout))
    gin, wg, gg, bg = pl.pallas_call(
        results,
        out_shape=(
            jax.ShapeDtypeStruct(inputs.shape, BF16),
            jax.ShapeDtypeStruct((3, 3, 8, cout), F32),
            jax.ShapeDtypeStruct((1, cout), F32),
            jax.ShapeDtypeStruct((1, cout), F32),
        ),
        in_specs=[any_spec, vmem_spec],
        out_specs=(any_spec, vmem_spec, vmem_spec, vmem_spec),
        scratch_shapes=[pltpu.VMEM((rows, cols, cin), BF16), dma((rows,)), dma((rows,))],
    )(gin, small)
    return gin, wg, gg.reshape(cout), bg.reshape(cout)


def solution(mesh):
    placed = (
        P("dp", "slab", None, None),
        P(),
        P("dp", "slab", None, None),
        P("dp", "slab", None, None),
        P(),
    )
    return jax.shard_map(
        per_device,
        mesh=mesh,
        in_specs=placed,
        out_specs=(P("dp", "slab", None, None), P(None, None, ("dp", "slab"), None), P(), P()),
        check_vma=False,
    )
```

```python
import functools

import jax
import jax.numpy as jnp
from jax import lax
from jax.experimental import pallas as pl
from jax.experimental.pallas import tpu as pltpu
from jax.sharding import PartitionSpec as P

MESH = pl.DeviceIdType.MESH
F32 = jnp.float32
BF16 = jnp.bfloat16
EPSILON = 1e-05
TAPS = ((1, 1), (0, 1), (2, 1), (1, 0), (1, 2), (0, 0), (0, 2), (2, 0), (2, 2))
GROUPS = ((0, 1, 2), (3, 4, 5), (6, 7, 8))


def kernel(
    sizes,
    x_hbm, w_hbm, pre_hbm, gn_hbm, gain_hbm,
    gin_ref, wg_ref, gg_ref, bg_ref,
    pre_v, gn_v, gain_v, st, xr, gr, xf, xc, gf, gc, wv, gin_v,
    dw, crecv, ssend, srecv, zsend, zrecv,
    gb, gbc, gbk, gbx, gbz,
    load_sem, w_sem, x_loc, gin_sem,
    st_s, st_r, x_s, x_r, g_s, g_r, c_s, c_r, s_s, s_r, z_s, z_r,
    gc_s, gc_r, gl_s, gl_r, gz_s, gz_r,
):
    ns, nz, rows, cols, cin, cout = sizes
    gran = cin // (2 * ns)
    pad = xf.shape[1]
    side = xc.shape[1]
    third = cols // 3
    cells = rows * cols * ns
    slab = lax.axis_index("slab")
    dp = lax.axis_index("dp")
    core = lax.rem(dp, 2)
    z = lax.rem(lax.div(dp, 2), nz)
    xlo = lax.div(dp, 2 * nz)
    other_core = {"dp": dp + 1 - 2 * core, "slab": slab}
    other_x = {"dp": dp + (1 - 2 * xlo) * (2 * nz), "slab": slab}
    nt = len(TAPS)

    def peer(q):
        return lax.rem(slab + q, ns)

    def source(q):
        return lax.rem(slab + ns - q, ns)

    def image_device(q):
        return {"dp": dp, "slab": peer(q)}

    def z_peer(q):
        return lax.rem(z + q, nz)

    def z_device(q):
        return {"dp": (xlo * nz + z_peer(q)) * 2 + core, "slab": slab}

    def pair_device(e, q):
        return {"dp": (xlo + e * (1 - 2 * xlo)) * (2 * nz) + lax.rem(dp, 2 * nz), "slab": peer(q)}

    pair_steps = [(e, q) for e in range(2) for q in range(ns) if e or q]

    loads = [
        pltpu.make_async_copy(pre_hbm.at[0], pre_v, load_sem.at[0]),
        pltpu.make_async_copy(gn_hbm.at[0], gn_v, load_sem.at[1]),
        pltpu.make_async_copy(gain_hbm, gain_v, load_sem.at[2]),
    ]
    for c in loads:
        c.start()

    barrier = pltpu.get_barrier_semaphore()
    friends = [image_device(q) for q in range(1, ns)] + [other_core, other_x]
    friends += [z_device(q) for q in range(1, nz)]
    for friend in friends:
        pl.semaphore_signal(barrier, inc=1, device_id=friend, device_id_type=MESH)

    half = lax.div(slab, ns // 2)
    part = lax.rem(slab + ns // 2, ns)
    row_tap = 2 * half
    weights = [
        pltpu.make_async_copy(w_hbm.at[1], wv.at[0], w_sem.at[0]),
        pltpu.make_async_copy(w_hbm.at[row_tap], wv.at[1], w_sem.at[1]),
    ]

    def lanes(a, s):
        return pl.ds(pl.multiple_of(a * (cin // 2) + s * gran, gran), gran)

    own_x = [
        pltpu.make_async_copy(
            x_hbm.at[0, :, :, lanes(a, slab)],
            xr.at[slab, :, :, pl.ds(a * gran, gran)],
            x_loc.at[a],
        )
        for a in range(2)
    ]

    for c in loads:
        c.wait()
    saved = pre_v[...].astype(F32)
    up = gn_v[...].astype(F32)

    def total(v):
        return jnp.sum(jnp.sum(v, axis=0), axis=0, keepdims=True)

    s1 = total(saved)
    centred = saved - s1 / (rows * cols)
    own_stats = [s1, total(centred * centred), total(up), total(up * centred)]
    st[slab] = jnp.concatenate(own_stats + [jnp.zeros((4, cout), F32)], axis=0)
    pl.semaphore_wait(barrier, len(friends))

    sends = []

    def send(src, dst, s_sem, r_sem, device):
        c = pltpu.make_async_remote_copy(
            src_ref=src, dst_ref=dst, send_sem=s_sem, recv_sem=r_sem,
            device_id=device, device_id_type=MESH,
        )
        c.start()
        sends.append(c)
        return c

    st_copies = [
        send(st.at[slab], st.at[slab], st_s.at[q], st_r.at[q], image_device(q))
        for q in range(1, ns)
    ]
    x_copies = {}
    for q in range(1, ns):
        for a in range(2):
            x_copies[q, a] = send(
                x_hbm.at[0, :, :, lanes(a, peer(q))],
                xr.at[slab, :, :, pl.ds(a * gran, gran)],
                x_s.at[q, a], x_r.at[q, a], image_device(q),
            )
    for c in own_x + weights:
        c.start()
    xf[:, side * 2 :, :] = jnp.zeros((ns * rows, pad - 2 * side, 2 * gran), BF16)
    gf[:, side * 2 :, :] = jnp.zeros((ns * rows, pad - 2 * side, cout), BF16)
    xc[...] = jnp.zeros(xc.shape, BF16)
    gc[...] = jnp.zeros(gc.shape, BF16)

    for c in st_copies:
        c.wait_recv()
    every = st[...]
    mean = jnp.sum(every[:, 0:1], axis=0) / cells
    m2 = jnp.zeros((1, cout), F32)
    sum_g = jnp.zeros((1, cout), F32)
    sum_gc = jnp.zeros((1, cout), F32)
    for k in range(ns):
        off = every[k, 0:1] / (rows * cols) - mean
        m2 = m2 + every[k, 1:2] + (rows * cols) * off * off
        sum_g = sum_g + every[k, 2:3]
        sum_gc = sum_gc + every[k, 3:4] + every[k, 2:3] * off
    inv_std = lax.rsqrt(m2 / cells + EPSILON)
    sum_gz = sum_gc * inv_std
    zhat = (saved - mean) * inv_std
    grad = (gain_v[...] * inv_std) * (up - sum_g / cells - zhat * (sum_gz / cells))
    gr[slab] = grad.astype(BF16)
    g_order = [ns // 2] + [q for q in range(1, ns) if q != ns // 2]
    g_copies = {
        q: send(gr.at[slab], gr.at[slab], g_s.at[q], g_r.at[q], image_device(q)) for q in g_order
    }
    gb[...] = jnp.concatenate([sum_gz, sum_g, jnp.zeros((6, cout), F32)], axis=0)
    gbc_copy = send(gb, gbc, gc_s, gc_r, other_core)

    def unpack(block, full, corner, k):
        v = block[k]
        at = pl.ds(k * rows, rows)
        full[at, 0:cols, :] = v
        corner[at, 0:third, :] = v[:, cols - third :, :]

    unpack(gr, gf, gc, slab)
    for c in own_x:
        c.wait()
    unpack(xr, xf, xc, slab)

    gbc_copy.wait_recv()
    gbk[...] = gb[...] + gbc[...]
    gbx_copy = send(gbk, gbx, gl_s, gl_r, other_x)

    for q in range(1, ns):
        x_copies[q, 0].wait_recv()
        x_copies[q, 1].wait_recv()
        unpack(xr, xf, xc, source(q))
    gbx_copy.wait_recv()
    gbz[z] = gbk[...] + gbx[...]
    gbz_copies = [
        send(gbz.at[z], gbz.at[z], gz_s.at[q], gz_r.at[q], z_device(q)) for q in range(1, nz)
    ]

    hh = ns * rows // 2

    def weight_tap(t):
        i, j = TAPS[t]
        h0, h1 = ((0, hh), (0, 2 * hh), (hh, 2 * hh))[i]
        g0, g1 = ((hh, 2 * hh), (0, 2 * hh), (0, hh))[i]
        xs = (xf[h0:h1, 0:side], xf[h0:h1], xc[h0:h1])[j]
        gs = (gc[g0:g1], gf[g0:g1], gf[g0:g1, 0:side])[j]
        n = xs.shape[0] * xs.shape[1]
        prod = lax.dot_general(
            xs.reshape(n, 2 * gran), gs.reshape(n, cout),
            (((0,), (0,)), ((), ())), preferred_element_type=F32,
        )
        dw[t] = prod.reshape(2, 2, gran // 2, cout)
        return send(
            dw.at[t, :, 1 - core], crecv.at[t], c_s.at[t], c_r.at[t], other_core
        )

    def core_stage(t, copy):
        copy.wait_recv()
        v = (dw[t, :, core] + crecv[t]).reshape(2, ns, 8, cout)
        v = jnp.concatenate([v[:, :, :, : cout // 2], v[:, :, :, cout // 2 :]], axis=2)
        ssend[:, :, t] = v.astype(BF16)

    def pair_send(g):
        at = pl.ds(GROUPS[g][0], len(GROUPS[g]))
        copies = []
        for e, q in pair_steps:
            to_x = xlo + e * (1 - 2 * xlo)
            copies.append(
                send(
                    ssend.at[to_x, peer(q), at], srecv.at[xlo, slab, at],
                    s_s.at[g, e, q], s_r.at[g, e, q], pair_device(e, q),
                )
            )
        srecv[xlo, slab, at] = ssend[xlo, slab, at]
        return copies

    def z_send(g, copies):
        for c in copies:
            c.wait_recv()
        at = pl.ds(GROUPS[g][0], len(GROUPS[g]))
        zsend[:, at] = (srecv[0, :, at].astype(F32) + srecv[1, :, at].astype(F32)).astype(BF16)
        out = [
            send(zsend.at[z_peer(q), at], zrecv.at[z, at], z_s.at[g, q], z_r.at[g, q], z_device(q))
            for q in range(1, nz)
        ]
        zrecv[z, at] = zsend[z, at]
        return out

    chunk = 256 if cin % 256 == 0 else cin

    def input_chunk(n, carry):
        at = pl.ds(pl.multiple_of(n * chunk, chunk), chunk)

        def prod(g, w):
            m = g.shape[0] * g.shape[1]
            return lax.dot_general(
                g.reshape(m, cout), w, (((1,), (1,)), ((), ())), preferred_element_type=F32
            ).reshape(g.shape[0], g.shape[1], chunk)

        mine, theirs = pl.ds(slab * rows, rows), pl.ds(part * rows, rows)
        mid = prod(gf[mine], wv[0, 1, at]) + prod(gf[theirs], wv[1, 1, at])
        first = prod(gc[mine], wv[0, 0, at]) + prod(gc[theirs], wv[1, 0, at])
        last = prod(gf[mine, 0:side], wv[0, 2, at]) + prod(gf[theirs, 0:side], wv[1, 2, at])
        tail = cols - third
        gin_v[:, :, at] = jnp.concatenate(
            [
                mid[:, :side] + first,
                mid[:, side:tail],
                mid[:, tail:cols] + last[:, :third],
            ],
            axis=1,
        ).astype(BF16)
        return carry

    for q in g_order:
        g_copies[q].wait_recv()
        unpack(gr, gf, gc, source(q))

    ng = len(GROUPS)
    c_copies, s_copies, z_copies = {}, {}, {}
    for step in range(ng + 2):
        if step < ng:
            for t in GROUPS[step]:
                c_copies[t] = weight_tap(t)
        if 1 <= step <= ng:
            for t in GROUPS[step - 1]:
                core_stage(t, c_copies[t])
            s_copies[step - 1] = pair_send(step - 1)
        if step == 2:
            for c in weights:
                c.wait()
        if step >= 2:
            done = (step - 2) * (cin // chunk) // ng
            lax.fori_loop(done, (step - 1) * (cin // chunk) // ng, input_chunk, 0)
        if step == ng + 1:
            gin_copy = pltpu.make_async_copy(gin_v, gin_ref.at[0], gin_sem)
            gin_copy.start()
        if step >= 2:
            z_copies[step - 2] = z_send(step - 2, s_copies[step - 2])

    for c in gbz_copies:
        c.wait_recv()
    both = jnp.sum(gbz[...], axis=0)
    gg_ref[...] = both[0:1]
    bg_ref[...] = both[1:2]
    for g in range(ng):
        for c in z_copies[g]:
            c.wait_recv()
        at = pl.ds(GROUPS[g][0], len(GROUPS[g]))
        acc = zrecv[0, at].astype(F32)
        for k in range(1, nz):
            acc = acc + zrecv[k, at].astype(F32)
        acc = jnp.concatenate([acc[:, :8], acc[:, 8:]], axis=2)
        for n, t in enumerate(GROUPS[g]):
            wg_ref[TAPS[t]] = acc[n]
    for c in sends:
        c.wait_send()
    gin_copy.wait()


def results(gin_in, wg_in, gg_in, bg_in, gin_ref, wg_ref, gg_ref, bg_ref, held, in_sem, out_sem, sem):
    rows = held.shape[0]
    into = [
        pltpu.make_async_copy(gin_in.at[0, r], held.at[r], in_sem.at[r]) for r in range(rows)
    ]
    out = [
        pltpu.make_async_copy(held.at[r], gin_ref.at[0, r], out_sem.at[r]) for r in range(rows)
    ]
    small = [
        pltpu.make_async_copy(wg_in.at[i], wg_ref.at[i], sem.at[i]) for i in range(3)
    ] + [
        pltpu.make_async_copy(gg_in, gg_ref, sem.at[3]),
        pltpu.make_async_copy(bg_in, bg_ref, sem.at[4]),
    ]
    for c in into + small:
        c.start()
    for r in range(rows):
        into[r].wait()
        out[r].start()
    for c in small + out:
        c.wait()


def per_device(inputs, weight, pre_norm, grad_norm, norm_gain):
    ns = lax.axis_size("slab")
    nz = lax.axis_size("dp") // 4
    _, rows, cols, cin = inputs.shape
    cout = pre_norm.shape[3]
    sizes = (ns, nz, rows, cols, cin, cout)
    block = 2 * (cin // (2 * ns))
    height = ns * rows
    pad, side = 48, 16
    nt, ng = len(TAPS), len(GROUPS)
    dma = pltpu.SemaphoreType.DMA
    any_spec = pl.BlockSpec(memory_space=pl.ANY)
    vmem_spec = pl.BlockSpec(memory_space=pltpu.VMEM)
    scratch = [
        pltpu.VMEM((rows, cols, cout), BF16),
        pltpu.VMEM((rows, cols, cout), BF16),
        pltpu.VMEM((1, cout), F32),
        pltpu.VMEM((ns, 8, cout), F32),
        pltpu.VMEM((ns, rows, cols, block), BF16),
        pltpu.VMEM((ns, rows, cols, cout), BF16),
        pltpu.VMEM((height, pad, block), BF16),
        pltpu.VMEM((height, side, block), BF16),
        pltpu.VMEM((height, pad, cout), BF16),
        pltpu.VMEM((height, side, cout), BF16),
        pltpu.VMEM((2, 3, cin, cout), BF16),
        pltpu.VMEM((rows, cols, cin), BF16),
        pltpu.VMEM((nt, 2, 2, block // 4, cout), F32),
        pltpu.VMEM((nt, 2, block // 4, cout), F32),
        pltpu.VMEM((2, ns, nt, 16, cout // 2), BF16),
        pltpu.VMEM((2, ns, nt, 16, cout // 2), BF16),
        pltpu.VMEM((nz, nt, 16, cout // 2), BF16),
        pltpu.VMEM((nz, nt, 16, cout // 2), BF16),
        pltpu.VMEM((8, cout), F32),
        pltpu.VMEM((8, cout), F32),
        pltpu.VMEM((8, cout), F32),
        pltpu.VMEM((8, cout), F32),
        pltpu.VMEM((nz, 8, cout), F32),
        dma((3,)), dma((2,)), dma((2,)), dma,
        dma((ns,)), dma((ns,)), dma((ns, 2)), dma((ns, 2)), dma((ns,)), dma((ns,)),
        dma((nt,)), dma((nt,)), dma((ng, 2, ns)), dma((ng, 2, ns)), dma((ng, nz)), dma((ng, nz)),
        dma, dma, dma, dma, dma((nz,)), dma((nz,)),
    ]
    shapes = (
        jax.ShapeDtypeStruct(inputs.shape, BF16),
        jax.ShapeDtypeStruct((3, 3, 8, cout), F32),
        jax.ShapeDtypeStruct((1, cout), F32),
        jax.ShapeDtypeStruct((1, cout), F32),
    )
    staged = pl.pallas_call(
        functools.partial(kernel, sizes),
        out_shape=shapes,
        in_specs=[any_spec] * 5,
        out_specs=(any_spec, vmem_spec, vmem_spec, vmem_spec),
        scratch_shapes=scratch,
        compiler_params=pltpu.CompilerParams(
            collective_id=0, has_side_effects=True, vmem_limit_bytes=56 * 1024 * 1024
        ),
    )(inputs, weight, pre_norm, grad_norm, norm_gain.reshape(1, cout))
    gin, wg, gg, bg = pl.pallas_call(
        results,
        out_shape=shapes,
        in_specs=[any_spec] * 4,
        out_specs=(any_spec,) * 4,
        scratch_shapes=[
            pltpu.VMEM((rows, cols, cin), BF16), dma((rows,)), dma((rows,)), dma((5,))
        ],
    )(*staged)
    return gin, wg, gg.reshape(cout), bg.reshape(cout)


def solution(mesh):
    placed = (
        P("dp", "slab", None, None),
        P(),
        P("dp", "slab", None, None),
        P("dp", "slab", None, None),
        P(),
    )
    return jax.shard_map(
        per_device,
        mesh=mesh,
        in_specs=placed,
        out_specs=(P("dp", "slab", None, None), P(None, None, ("dp", "slab"), None), P(), P()),
        check_vma=False,
    )
```
